32 devices in a mesh: grp: 2 (over x), pts: 16 (over z, y, core).
Axes of the slice: x: 2, y: 2, z: 4, core: 2. Of those that a mesh axis runs over, the one named last changes fastest.
Arguments:
- spectrum: float32 [1296, 8192], P(None, ('grp', 'pts')), parts along dimension 1, may hold values from 0.01 to 29, as said below
- wind_speed: float32 [8192], P(('grp', 'pts')), parts along dimension 0, may hold values from 0.5 to 3
- wind_dir: float32 [8192], P(('grp', 'pts')), parts along dimension 0, may hold values from -3.140625 to 3.140625
- turning: float32 [8192], P(('grp', 'pts')), parts along dimension 0, may hold values from -0.8 to 0.8
- sea_mask: int32 [48, 128], P('pts'), may hold values from 0 to 1, as said below
- band_start: int32 [16], replicated, may hold values from 0 to 4095, as said below
Outputs:
- updated: float32 [1296, 8192], P(None, ('grp', 'pts')), parts along dimension 1
The draws below stay inside these ranges and needn't reach their ends.
There are 2 independent parts, one for each index of `grp`. The reference program is written for one: setup_inputs(seed, part) draws one part's arguments, and reference() takes and returns one part's arrays. A program takes and returns all parts, laid end to end along the dimension named above; an argument that names none is the same for every part. Nothing has to cross between parts.
Inputs may be any that keep to these rules, and one draw needn't show every extreme that they name: `spectrum`: spectrum entries are positive. `sea_mask`: there are exactly 4096 sea cells. Band b holds band_start[b + 1] - band_start[b] of them (the last band the rest up to 4096); every band holds at most 384 sea cells, and one band holds exactly that many. band_start[0] is 0 and band_start[b] is the number of sea cells in the rows before band b; every band holds at least one sea cell.
All inputs are finite; a program needn't handle non-finite values.
Results may differ from the reference program's by a relative error of at most 0.000076.
Values sent between devices are 32-bit elements; how exact they have to be, the bound alone decides.
A program may use at most 64 MiB of HBM per device.

```python
import math
import jax
import jax.numpy as jnp
from jax import lax

DIRS = 36
FREQS = 36
COMPONENTS = 1296
P_DEV = 256
ROWS_BAND = 3
LON_CELLS = 128
SEA = 4096
LAT_CELLS = 48
SLOTS = 24
N_PTS = 16


def ocean_layout(key):
    pair_key, chosen_key, perm_key, anchor_key, drift_key = jax.random.split(key, 5)
    half = N_PTS // 2
    band_cells = ROWS_BAND * LON_CELLS
    busiest = SLOTS * N_PTS
    spread = (busiest - P_DEV) * 3 // 4
    deltas = jax.random.randint(pair_key, (half,), 0, spread + 1).astype(jnp.int32)
    chosen = jax.random.randint(chosen_key, (), 0, half).astype(jnp.int32)
    deltas = jnp.where(jnp.arange(half, dtype=jnp.int32) == chosen, busiest - P_DEV, deltas).astype(jnp.int32)
    paired = jnp.concatenate([P_DEV + deltas, P_DEV - deltas]).astype(jnp.int32)
    shuffle = jax.random.permutation(perm_key, N_PTS)
    counts = paired[shuffle].astype(jnp.int32)
    land = band_cells - counts
    row_ids = jnp.arange(ROWS_BAND, dtype=jnp.int32)
    row_land = land[:, None] // ROWS_BAND + (row_ids[None, :] < (land % ROWS_BAND)[:, None]).astype(jnp.int32)
    row_land = row_land.reshape(-1).astype(jnp.int32)
    steps_drift = jax.random.randint(drift_key, (LAT_CELLS,), -6, 7).astype(jnp.int32)
    anchor = jax.random.randint(anchor_key, (), 0, LON_CELLS).astype(jnp.int32)
    first_land = (anchor + jnp.cumsum(steps_drift)) % LON_CELLS
    offset = (jnp.arange(LON_CELLS, dtype=jnp.int32)[None, :] - first_land[:, None]) % LON_CELLS
    mask = (offset >= row_land[:, None]).astype(jnp.int32)
    starts = (jnp.cumsum(counts) - counts).astype(jnp.int32)
    return (mask, starts)


def draw_sea_mask(key, part):
    mask, starts = ocean_layout(key)
    return mask


def draw_band_start(key, part):
    mask, starts = ocean_layout(key)
    return starts


def draw_spectrum(key, part):
    key = jax.random.fold_in(key, 11)
    comp_key, point_key, rough_key = jax.random.split(key, 3)
    lowest, highest, rough_lo, rough_hi = (0.3, 3.0, 0.5, 1.5)
    comp_scale = jnp.exp(jax.random.uniform(comp_key, (COMPONENTS, 1), jnp.float32, math.log(lowest), math.log(highest)))
    point_scale = jnp.exp(jax.random.uniform(point_key, (1, SEA), jnp.float32, math.log(lowest), math.log(highest)))
    rough = jax.random.uniform(rough_key, (COMPONENTS, SEA), jnp.float32, rough_lo, rough_hi)
    return (comp_scale * point_scale * rough).astype(jnp.float32)


def block_levels(rng, extent, cuts, smallest, high):
    gain, own = 1.0, jax.random.fold_in(rng, 6)
    for dim, parts in cuts:
        steps = jnp.exp(jax.random.uniform(jax.random.fold_in(own, dim), (parts,), jnp.float32, smallest / len(cuts), high / len(cuts)))
        gain = gain * jnp.repeat(steps, extent[dim] // parts).reshape([-1 if axis == dim else 1 for axis in range(len(extent))])
    return gain


def setup_inputs(seed: int = 0, part: int = 0) -> dict:
    key_of = jax.random.split(jax.random.key(seed), 7)
    own_keys = jax.random.split(jax.random.fold_in(key_of[6], part), 7)
    return {
        "spectrum": draw_spectrum(jax.random.fold_in(jax.random.fold_in(key_of[6], part), 71), part),
        "wind_speed": jnp.clip(jnp.exp(math.log(3.0) - 1.7917595 * jax.random.uniform(own_keys[1], (SEA,), jnp.float32) ** block_levels(own_keys[1], (SEA,), ((0, 16),), -0.2, 0.2)), 0.5, 3.0),
        "wind_dir": jnp.clip(jax.random.uniform(own_keys[2], (SEA,), jnp.float32, -3.140625, 3.140625), -3.140625, 3.140625),
        "turning": jnp.clip(jax.random.uniform(own_keys[3], (SEA,), jnp.float32, -0.8, 0.8) * block_levels(own_keys[3], (SEA,), ((0, 16),), -0.4, 0.0), -0.8, 0.8),
        "sea_mask": draw_sea_mask(jax.random.fold_in(key_of[6], 71), part),
        "band_start": draw_band_start(jax.random.fold_in(key_of[6], 71), part),
    }


def spectral_tables():
    freq_steps = jnp.arange(FREQS, dtype=jnp.float32) / (FREQS - 1)
    frequency = 0.5 + 1.5 * freq_steps
    heading = (2.0 * math.pi / DIRS) * jnp.arange(DIRS, dtype=jnp.float32)
    group_speed = 0.3 + 0.5 * freq_steps
    return frequency, heading, group_speed


def turning_matrix():
    row_ids = jnp.arange(DIRS)[:, None]
    col_ids = jnp.arange(DIRS)[None, :]
    ahead = (col_ids == (row_ids + 1) % DIRS).astype(jnp.float32)
    behind = (col_ids == (row_ids - 1) % DIRS).astype(jnp.float32)
    return 0.5 * ahead - 0.5 * behind


def source_terms(density, wind_speed, wind_dir, turning):
    frequency, heading, group_speed = spectral_tables()
    energy = jnp.mean(density, axis=0)
    shaped = density.reshape(FREQS, DIRS, -1)
    alignment = jnp.cos(heading[:, None] - wind_dir[None, :])
    growth = 0.2 * jax.nn.relu(wind_speed * alignment / frequency[:, None, None] - 0.3)
    decay = 0.1 * frequency[:, None, None] * energy
    sourced = shaped * jnp.exp(growth - decay)
    rotated = jnp.einsum("ts,fsx->ftx", turning_matrix(), sourced, precision=lax.Precision.HIGHEST)
    refracted = sourced - (turning / frequency[:, None, None]) * rotated
    return refracted.reshape(FREQS * DIRS, -1)


def advect(padded, cross, meridional):
    center = padded[:, 1:-1]
    south = padded[:, :-2]
    north = padded[:, 2:]
    western = jnp.roll(center, 1, axis=2)
    eastern = jnp.roll(center, -1, axis=2)
    return (center - jax.nn.relu(cross) * (center - western) - jnp.minimum(cross, 0.0) * (eastern - center)
            - jax.nn.relu(meridional) * (center - south) - jnp.minimum(meridional, 0.0) * (north - center))


def reference(spectrum, wind_speed, wind_dir, turning, sea_mask, band_start):
    refracted = source_terms(spectrum, wind_speed, wind_dir, turning).reshape(FREQS, DIRS, SEA)
    band_mask = sea_mask.reshape(N_PTS, ROWS_BAND * LON_CELLS)
    sea_index = (band_start[:, None] + jnp.cumsum(band_mask, axis=1) - 1).reshape(-1)
    column = jnp.clip((sea_index % N_PTS) * P_DEV + sea_index // N_PTS, 0, SEA - 1).astype(jnp.int32)
    sea_float = sea_mask.reshape(-1).astype(jnp.float32)
    sea_cells = jnp.nonzero(sea_mask.reshape(-1), size=SEA)[0].astype(jnp.int32)
    targets = column[sea_cells]
    frequency, heading, group_speed = spectral_tables()
    latitude = (-60.0 + 120.0 * (jnp.arange(LAT_CELLS, dtype=jnp.float32) + 0.5) / LAT_CELLS) * (math.pi / 180.0)

    def one_frequency(payload):
        freq_index, block = payload
        grid = (jnp.take(block, column, axis=1) * sea_float).reshape(DIRS, LAT_CELLS, LON_CELLS)
        padded = jnp.pad(grid, ((0, 0), (1, 1), (0, 0)))
        along = (0.4 * group_speed[freq_index]) * jnp.cos(heading)
        across = (0.35 * group_speed[freq_index]) * jnp.sin(heading)
        cross = (along[:, None] / jnp.cos(latitude)[None, :])[:, :, None]
        advanced = advect(padded, cross, across[:, None, None]).reshape(DIRS, -1)
        return jnp.zeros((DIRS, SEA), jnp.float32).at[:, targets].set(advanced[:, sea_cells])

    result = lax.map(one_frequency, (jnp.arange(FREQS), refracted))
    return result.reshape(FREQS * DIRS, SEA)
```

```python
import functools
import math

import jax
import jax.numpy as jnp
import numpy as np
from jax import lax
from jax.experimental import pallas as pl
from jax.experimental.pallas import tpu as pltpu
from jax.sharding import PartitionSpec as P

DIRS = 36
FREQS = 36
PAIR = 2 * DIRS
LANES = 128
CHUNK = 16
MESH = pl.DeviceIdType.MESH


def spectral_tables():
    heading = 2.0 * np.pi / DIRS * np.arange(DIRS)
    group_speed = 0.3 + 0.5 * np.arange(FREQS) / (FREQS - 1)
    along = ((0.4 * group_speed)[:, None] * np.cos(heading)[None, :]).reshape(-1, 1)
    across = ((0.35 * group_speed)[:, None] * np.sin(heading)[None, :]).reshape(-1, 1)
    wide = lambda v, lanes: np.ascontiguousarray(np.broadcast_to(v, (v.shape[0], lanes))).astype(np.float32)
    cos2 = np.tile(np.cos(heading), 2)[:, None]
    sin2 = np.tile(np.sin(heading), 2)[:, None]
    ids = np.arange(DIRS)
    turn = 0.5 * (ids[None, :] == (ids[:, None] + 1) % DIRS) - 0.5 * (ids[None, :] == (ids[:, None] - 1) % DIRS)
    turn2 = np.kron(np.eye(2), turn).astype(np.float32)
    return wide(along, LANES), wide(across, LANES), wide(cos2, LANES), wide(sin2, LANES), turn2


def lane_take(x, idx):
    return jnp.take_along_axis(x, idx, axis=1, mode="promise_in_bounds")


def granule_transpose(tiles, granule, lane):
    tiles = list(tiles)
    step = 1
    while step < len(tiles):
        keep = (lane // granule) & step == 0
        for d in range(len(tiles)):
            if d & step == 0:
                a, b = tiles[d], tiles[d | step]
                width = step * granule
                tiles[d] = jnp.where(keep, a, pltpu.roll(b, width, 1))
                tiles[d | step] = jnp.where(keep, pltpu.roll(a, LANES - width, 1), b)
        step *= 2
    return tiles


def kernel(n, spec, speed, wdir, turning, mask, along, across, cos2, sin2, turn2, lat,
           out, refr, arrived, result, ex_in, ex_out, aligned, slots, cells, rolled, tabs, lat_tab, grid,
           mask_send, mask_recv, fwd_send, fwd_recv, back_send, back_recv,
           exf_send, exf_recv, exb_send, exb_recv):
    me = lax.axis_index("pts")
    comps, points = spec.shape
    band_rows = mask.shape[0]
    rows = band_rows * n
    tiles = points * n // LANES
    halves = points // LANES
    granule = LANES // n
    log_n = n.bit_length() - 1
    groups = comps // 8
    per_dev = groups // n * 8
    chunks = per_dev // CHUNK
    extra = groups - n * (per_dev // 8)
    base = 8 * extra

    def peer(i):
        return lax.rem(me + i, n)

    def each_peer(body):
        def step(i, carry):
            body(peer(i))
            return carry
        lax.fori_loop(1, n, step, 0)

    def remote(src, dst, send, recv, dev):
        return pltpu.make_async_remote_copy(src_ref=src, dst_ref=dst, send_sem=send, recv_sem=recv,
                                            device_id={"pts": dev}, device_id_type=MESH)

    def wait_bytes(ref, sem):
        pltpu.make_async_copy(ref, ref, sem).wait()

    def rows_of(start, count):
        return pl.ds(pl.multiple_of(start, 8), count)

    barrier = pltpu.get_barrier_semaphore()
    each_peer(lambda p: pl.semaphore_signal(barrier, inc=1, device_id={"pts": p}, device_id_type=MESH))
    slots[me] = jnp.zeros((8, LANES), jnp.float32)
    slots[me, 0:band_rows, :] = mask[...].astype(jnp.float32)

    cos_w = speed[...] * jnp.cos(wdir[...])
    sin_w = speed[...] * jnp.sin(wdir[...])
    aligned[...] = cos2[:, 0:1] * cos_w + sin2[:, 0:1] * sin_w
    energy = jnp.sum(spec[...].reshape(comps // 8, 8, points), axis=0)
    energy = jnp.sum(energy, axis=0, keepdims=True) * (0.1 / comps)
    turn_col = turning[...]
    second = lax.broadcasted_iota(jnp.int32, (PAIR, points), 0) >= DIRS

    pl.semaphore_wait(barrier, n - 1)
    each_peer(lambda p: remote(slots.at[me], slots.at[me], mask_send, mask_recv, p).start())

    def source(i, carry):
        at = rows_of(i * PAIR, PAIR)
        freq = 0.5 + (3.0 / (FREQS - 1)) * i.astype(jnp.float32)
        sigma = jnp.where(second, freq + 1.5 / (FREQS - 1), freq)
        inv = 1.0 / sigma
        growth = 0.2 * jnp.maximum(aligned[...] * inv - 0.3, 0.0)
        x = spec[at, :] * jnp.exp(growth - sigma * energy)
        rot = jnp.dot(turn2[...], x, precision=lax.Precision.HIGHEST, preferred_element_type=jnp.float32)
        refr[at, :] = x - turn_col * inv * rot
        return carry

    done = 0

    def source_to(row_end, done):
        need = -(-row_end // PAIR)
        if need > done:
            lax.fori_loop(done, need, source, 0)
        return max(need, done)

    done = source_to(base, done)
    for p in range(extra):
        @pl.when(me != p)
        def _():
            remote(refr.at[pl.ds(8 * p, 8)], ex_in.at[me], exf_send.at[p], exf_recv, p).start()

        @pl.when(me == p)
        def _():
            ex_in[me] = refr[8 * p:8 * p + 8, :]
    for c in range(chunks):
        first = base + c * CHUNK * n
        done = source_to(first + CHUNK * n, done)
        each_peer(lambda p: remote(refr.at[rows_of(first + CHUNK * p, CHUNK)], arrived.at[c, me],
                                   fwd_send.at[c], fwd_recv.at[c], p).start())
        arrived[c, me] = refr[rows_of(first + CHUNK * me, CHUNK), :]

    others = pl.ds(0, n - 1)
    wait_bytes(slots.at[others], mask_recv)
    for b in range(n):
        cells[band_rows * b:band_rows * (b + 1), :] = slots[b, 0:band_rows, :]
    m = cells[...]
    tri = (lax.broadcasted_iota(jnp.int32, (LANES, LANES), 0)
           < lax.broadcasted_iota(jnp.int32, (LANES, LANES), 1)).astype(jnp.float32)
    low = (lax.broadcasted_iota(jnp.int32, (rows, rows), 1)
           < lax.broadcasted_iota(jnp.int32, (rows, rows), 0)).astype(jnp.float32)
    rank = jnp.dot(m, tri, preferred_element_type=jnp.float32).astype(jnp.int32)
    before = jnp.dot(low, m, preferred_element_type=jnp.float32)
    begin = jnp.broadcast_to(jnp.sum(before, axis=1, keepdims=True), m.shape).astype(jnp.int32)
    count = jnp.broadcast_to(jnp.sum(m, axis=1, keepdims=True), m.shape).astype(jnp.int32)
    sea = m > 0.5
    lane = lax.broadcasted_iota(jnp.int32, (rows, LANES), 1)
    row = lax.broadcasted_iota(jnp.int32, (rows, LANES), 0)
    index = jnp.where(sea, begin + rank, -1)
    west = pltpu.roll(index, 1, 1)
    east = pltpu.roll(index, LANES - 1, 1)
    south = jnp.where(row == 0, -1, pltpu.roll(index, 1, 0))
    north = jnp.where(row == rows - 1, -1, pltpu.roll(index, rows - 1, 0))
    col = jnp.where(sea, lane, -1)
    shift = jnp.where(sea, lane - rank, 0)
    for bit in range(7):
        width = 1 << bit
        col_m = pltpu.roll(col, LANES - width, 1)
        shift_m = pltpu.roll(shift, LANES - width, 1)
        take = (col_m >= 0) & (((shift_m >> bit) & 1) == 1)
        stay = (col >= 0) & (((shift >> bit) & 1) == 0)
        col = jnp.where(take, col_m, jnp.where(stay, col, -1))
        shift = jnp.where(take, shift_m, shift)
    source_col = jnp.maximum(lane_take(col, (lane - begin) & (LANES - 1)), 0)
    for i, table in enumerate((west, east, south, north)):
        rolled[i] = lane_take(table, source_col)
    rolled[4] = begin
    rolled[5] = begin + count

    q_tile = lax.broadcasted_iota(jnp.int32, (tiles, LANES), 0)
    q_lane = lax.broadcasted_iota(jnp.int32, (tiles, LANES), 1)
    q = q_tile * LANES + q_lane

    def spread(r, carry):
        at = pl.ds(r, 1)
        inside = (q >= rolled[4, at, :]) & (q < rolled[5, at, :])
        pieces = [jnp.where(inside, rolled[i, at, :], carry[i]) for i in range(4)]
        return (*pieces, jnp.where(inside, lat[at, :], carry[4]))

    zero = jnp.zeros((tiles, LANES), jnp.int32)
    found = lax.fori_loop(0, rows, spread, (zero, zero, zero, zero, zero.astype(jnp.float32)))
    order = (q_lane & (granule - 1)) * n + q_lane // granule
    for i in range(4):
        near = found[i]
        code = (((near >> 7) - q_tile + 1) * LANES + granule * (near & (n - 1))
                + ((near & (LANES - 1)) >> log_n))
        code = lane_take(jnp.where(near < 0, 3 * LANES, code), order)
        for t in range(tiles):
            tabs[t, i] = jnp.broadcast_to(code[t:t + 1, :], (8, LANES))
    inverse_lat = lane_take(found[4], order)
    for t in range(tiles):
        lat_tab[t] = jnp.broadcast_to(inverse_lat[t:t + 1, :], (8, LANES))

    lane8 = lax.broadcasted_iota(jnp.int32, (8, LANES), 1)

    def advance(src, dst, sub, first_row):
        at = pl.ds(8 * sub, 8)
        for h in range(halves):
            part = pl.ds(h * LANES, LANES)
            moved = granule_transpose([src[d, at, part] for d in range(n)], granule, lane8)
            for t in range(n):
                grid[sub, h * n + t] = moved[t]
        zonal = along[rows_of(first_row, 8), :]
        merid = across[rows_of(first_row, 8), :]
        from_west = zonal > 0.0
        from_south = merid > 0.0
        zonal, merid = jnp.abs(zonal), jnp.abs(merid)

        def pick(code, prev, cur, nxt):
            where = code & (LANES - 1)
            tile = code >> 7
            got = jnp.where(tile == 1, lane_take(cur, where), 0.0)
            got = jnp.where(tile == 0, lane_take(prev, where), got)
            return jnp.where(tile == 2, lane_take(nxt, where), got)

        for h in range(halves):
            new = []
            for u in range(n):
                t = h * n + u
                prev, cur, nxt = grid[sub, max(t - 1, 0)], grid[sub, t], grid[sub, min(t + 1, tiles - 1)]
                beside = pick(jnp.where(from_west, tabs[t, 0], tabs[t, 1]), prev, cur, nxt)
                behind = pick(jnp.where(from_south, tabs[t, 2], tabs[t, 3]), prev, cur, nxt)
                new.append(cur - zonal * lat_tab[t] * (cur - beside) - merid * (cur - behind))
            moved = granule_transpose(new, granule, lane8)
            part = pl.ds(h * LANES, LANES)
            for d in range(n):
                dst[d, at, part] = moved[d]

    if extra:
        @pl.when(me < extra)
        def _():
            wait_bytes(ex_in.at[others], exf_recv)
            advance(ex_in, ex_out, 0, 8 * me)
            each_peer(lambda p: remote(ex_out.at[p], out.at[rows_of(8 * me, 8)], exb_send, exb_recv.at[me], p).start())
            out[rows_of(8 * me, 8), :] = ex_out[me]

    def one_chunk(c, carry):
        wait_bytes(arrived.at[c, others], fwd_recv.at[c])
        mine = base + c * CHUNK * n + CHUNK * me
        for sub in range(CHUNK // 8):
            advance(arrived.at[c], result.at[c], sub, mine + 8 * sub)
        each_peer(lambda p: remote(result.at[c, p], out.at[rows_of(mine, CHUNK)],
                                   back_send.at[c], back_recv.at[c], p).start())
        out[rows_of(mine, CHUNK), :] = result[c, me]
        return carry

    lax.fori_loop(0, chunks, one_chunk, 0)

    wait_bytes(slots.at[others], mask_send)
    for c in range(chunks):
        wait_bytes(arrived.at[c, others], fwd_send.at[c])
        wait_bytes(result.at[c, others], back_send.at[c])
        wait_bytes(result.at[c, others], back_recv.at[c])
    if extra:
        for p in range(extra):
            @pl.when(me != p)
            def _():
                wait_bytes(ex_in.at[0], exf_send.at[p])
                wait_bytes(ex_in.at[0], exb_recv.at[p])

        @pl.when(me < extra)
        def _():
            wait_bytes(ex_out.at[others], exb_send)


def shards(n, spectrum, wind_speed, wind_dir, turning, sea_mask, band_start):
    comps, points = spectrum.shape
    band_rows = sea_mask.shape[0]
    rows = band_rows * n
    tiles = points * n // LANES
    groups = comps // 8
    chunks = max(groups // n * 8 // CHUNK, 1)
    extra = max(groups - n * (groups // n), 1)
    latitude = (-60.0 + 120.0 * (np.arange(rows) + 0.5) / rows) * (math.pi / 180.0)
    lat = np.ascontiguousarray(np.broadcast_to((1.0 / np.cos(latitude))[:, None], (rows, LANES))).astype(np.float32)
    vmem = pl.BlockSpec(memory_space=pltpu.VMEM)
    dma = pltpu.SemaphoreType.DMA
    f32, i32 = jnp.float32, jnp.int32
    call = pl.pallas_call(
        functools.partial(kernel, n),
        out_shape=jax.ShapeDtypeStruct((comps, points), f32),
        in_specs=[vmem] * 11,
        out_specs=vmem,
        scratch_shapes=[
            pltpu.VMEM((comps, points), f32),
            pltpu.VMEM((chunks, n, CHUNK, points), f32),
            pltpu.VMEM((chunks, n, CHUNK, points), f32),
            pltpu.VMEM((n, 8, points), f32),
            pltpu.VMEM((n, 8, points), f32),
            pltpu.VMEM((PAIR, points), f32),
            pltpu.VMEM((n, 8, LANES), f32),
            pltpu.VMEM((rows, LANES), f32),
            pltpu.VMEM((6, rows, LANES), i32),
            pltpu.VMEM((tiles, 4, 8, LANES), i32),
            pltpu.VMEM((tiles, 8, LANES), f32),
            pltpu.VMEM((CHUNK // 8, tiles, 8, LANES), f32),
            dma, dma,
            dma((chunks,)), dma((chunks,)), dma((chunks,)), dma((chunks,)),
            dma((extra,)), dma, dma, dma((extra,)),
        ],
        compiler_params=pltpu.CompilerParams(
            collective_id=0, has_side_effects=True, vmem_limit_bytes=40 * 1024 * 1024
        ),
    )
    line = lambda v: v.reshape(1, points)
    return call(spectrum, line(wind_speed), line(wind_dir), line(turning), sea_mask, *spectral_tables(), lat)


def solution(mesh):
    placed = (
        P(None, ("grp", "pts")),
        P(("grp", "pts")),
        P(("grp", "pts")),
        P(("grp", "pts")),
        P("pts", None),
        P(),
    )
    return jax.shard_map(
        functools.partial(shards, mesh.shape["pts"]), mesh=mesh, in_specs=placed,
        out_specs=P(None, ("grp", "pts")), check_vma=False
    )
```

```python
import functools
import math

import jax
import jax.numpy as jnp
import numpy as np
from jax import lax
from jax.experimental import pallas as pl
from jax.experimental.pallas import tpu as pltpu
from jax.sharding import PartitionSpec as P

DIRS = 36
FREQS = 36
PAIR = 2 * DIRS
LANES = 128
CHUNK = 16
MESH = pl.DeviceIdType.MESH


def spectral_tables():
    heading = 2.0 * np.pi / DIRS * np.arange(DIRS)
    group_speed = 0.3 + 0.5 * np.arange(FREQS) / (FREQS - 1)
    along = ((0.4 * group_speed)[:, None] * np.cos(heading)[None, :]).reshape(-1, 1)
    across = ((0.35 * group_speed)[:, None] * np.sin(heading)[None, :]).reshape(-1, 1)
    wide = lambda v, lanes: np.ascontiguousarray(np.broadcast_to(v, (v.shape[0], lanes))).astype(np.float32)
    cos2 = np.tile(np.cos(heading), 2)[:, None]
    sin2 = np.tile(np.sin(heading), 2)[:, None]
    ids = np.arange(DIRS)
    turn = 0.5 * (ids[None, :] == (ids[:, None] + 1) % DIRS) - 0.5 * (ids[None, :] == (ids[:, None] - 1) % DIRS)
    turn2 = np.kron(np.eye(2), turn).astype(np.float32)
    return wide(along, LANES), wide(across, LANES), wide(cos2, LANES), wide(sin2, LANES), turn2


def lane_take(x, idx):
    return jnp.take_along_axis(x, idx, axis=1, mode="promise_in_bounds")


def granule_transpose(tiles, granule, lane):
    tiles = list(tiles)
    step = 1
    while step < len(tiles):
        keep = (lane // granule) & step == 0
        for d in range(len(tiles)):
            if d & step == 0:
                a, b = tiles[d], tiles[d | step]
                width = step * granule
                tiles[d] = jnp.where(keep, a, pltpu.roll(b, width, 1))
                tiles[d | step] = jnp.where(keep, pltpu.roll(a, LANES - width, 1), b)
        step *= 2
    return tiles


def kernel(n, spec_hbm, speed_hbm, wdir_hbm, turning_hbm, mask_hbm, along_hbm, across_hbm, cos2_hbm, sin2_hbm,
           turn2_hbm, lat_hbm, out, spec, speed, wdir, turning, mask, along, across, cos2, sin2, turn2, lat, loaded, refr, arrived, result, ex_in, ex_out, aligned, slots, cells, rolled, tabs, lat_tab, grid,
           mask_send, mask_recv, fwd_send, fwd_recv, back_send, back_recv,
           exf_send, exf_recv, exb_send, exb_recv):
    me = lax.axis_index("pts")
    comps, points = spec.shape
    band_rows = mask.shape[0]
    rows = band_rows * n
    tiles = points * n // LANES
    halves = points // LANES
    granule = LANES // n
    log_n = n.bit_length() - 1
    groups = comps // 8
    per_dev = groups // n * 8
    chunks = per_dev // CHUNK
    extra = groups - n * (per_dev // 8)
    base = 8 * extra

    half = n // 2
    operands = {
        "mask": (mask_hbm, mask), "speed": (speed_hbm, speed), "wdir": (wdir_hbm, wdir),
        "turning": (turning_hbm, turning), "spec": (spec_hbm, spec), "cos2": (cos2_hbm, cos2),
        "sin2": (sin2_hbm, sin2), "turn2": (turn2_hbm, turn2), "lat": (lat_hbm, lat),
        "along": (along_hbm, along), "across": (across_hbm, across),
    }
    loads = {name: pltpu.make_async_copy(src, dst, loaded.at[i]) for i, (name, (src, dst)) in enumerate(operands.items())}
    for load in loads.values():
        load.start()

    def need(*names):
        for name in names:
            loads[name].wait()

    def each_peer(body):
        def far(i, carry):
            body(half * (1 - me // half) + lax.rem(me + i, half))
            return carry

        def near(i, carry):
            body(half * (me // half) + lax.rem(me + i, half))
            return carry

        lax.fori_loop(0, half, far, 0)
        lax.fori_loop(1, half, near, 0)

    def remote(src, dst, send, recv, dev):
        return pltpu.make_async_remote_copy(src_ref=src, dst_ref=dst, send_sem=send, recv_sem=recv,
                                            device_id={"pts": dev}, device_id_type=MESH)

    def wait_bytes(ref, sem):
        pltpu.make_async_copy(ref, ref, sem).wait()

    def rows_of(start, count):
        return pl.ds(pl.multiple_of(start, 8), count)

    barrier = pltpu.get_barrier_semaphore()
    each_peer(lambda p: pl.semaphore_signal(barrier, inc=1, device_id={"pts": p}, device_id_type=MESH))
    need("mask")
    slots[me] = jnp.zeros((8, LANES), jnp.float32)
    slots[me, 0:band_rows, :] = mask[...].astype(jnp.float32)

    need("speed", "wdir", "turning", "cos2", "sin2", "turn2")
    cos_w = speed[...] * jnp.cos(wdir[...])
    sin_w = speed[...] * jnp.sin(wdir[...])
    aligned[...] = cos2[:, 0:1] * cos_w + sin2[:, 0:1] * sin_w
    need("spec")
    energy = jnp.sum(spec[...].reshape(comps // 8, 8, points), axis=0)
    energy = jnp.sum(energy, axis=0, keepdims=True) * (0.1 / comps)
    turn_col = turning[...]
    second = lax.broadcasted_iota(jnp.int32, (PAIR, points), 0) >= DIRS

    pl.semaphore_wait(barrier, n - 1)
    each_peer(lambda p: remote(slots.at[me], slots.at[me], mask_send, mask_recv, p).start())

    def source(i, carry):
        at = rows_of(i * PAIR, PAIR)
        freq = 0.5 + (3.0 / (FREQS - 1)) * i.astype(jnp.float32)
        sigma = jnp.where(second, freq + 1.5 / (FREQS - 1), freq)
        inv = 1.0 / sigma
        growth = 0.2 * jnp.maximum(aligned[...] * inv - 0.3, 0.0)
        x = spec[at, :] * jnp.exp(growth - sigma * energy)
        rot = jnp.dot(turn2[...], x, precision=lax.Precision.HIGHEST, preferred_element_type=jnp.float32)
        refr[at, :] = x - turn_col * inv * rot
        return carry

    done = 0

    def source_to(row_end, done):
        end = -(-row_end // PAIR)
        if end > done:
            lax.fori_loop(done, end, source, 0)
        return max(end, done)

    done = source_to(base, done)
    for p in range(extra):
        @pl.when(me != p)
        def _():
            remote(refr.at[pl.ds(8 * p, 8)], ex_in.at[me], exf_send.at[p], exf_recv, p).start()

        @pl.when(me == p)
        def _():
            ex_in[me] = refr[8 * p:8 * p + 8, :]
    for c in range(chunks):
        first = base + c * CHUNK * n
        done = source_to(first + CHUNK * n, done)
        each_peer(lambda p: remote(refr.at[rows_of(first + CHUNK * p, CHUNK)], arrived.at[c, me],
                                   fwd_send.at[c], fwd_recv.at[c], p).start())
        arrived[c, me] = refr[rows_of(first + CHUNK * me, CHUNK), :]

    need("lat", "along", "across")
    others = pl.ds(0, n - 1)
    wait_bytes(slots.at[others], mask_recv)
    for b in range(n):
        cells[band_rows * b:band_rows * (b + 1), :] = slots[b, 0:band_rows, :]
    m = cells[...]
    tri = (lax.broadcasted_iota(jnp.int32, (LANES, LANES), 0)
           < lax.broadcasted_iota(jnp.int32, (LANES, LANES), 1)).astype(jnp.float32)
    low = (lax.broadcasted_iota(jnp.int32, (rows, rows), 1)
           < lax.broadcasted_iota(jnp.int32, (rows, rows), 0)).astype(jnp.float32)
    rank = jnp.dot(m, tri, preferred_element_type=jnp.float32).astype(jnp.int32)
    before = jnp.dot(low, m, preferred_element_type=jnp.float32)
    begin = jnp.broadcast_to(jnp.sum(before, axis=1, keepdims=True), m.shape).astype(jnp.int32)
    count = jnp.broadcast_to(jnp.sum(m, axis=1, keepdims=True), m.shape).astype(jnp.int32)
    sea = m > 0.5
    lane = lax.broadcasted_iota(jnp.int32, (rows, LANES), 1)
    row = lax.broadcasted_iota(jnp.int32, (rows, LANES), 0)
    index = jnp.where(sea, begin + rank, -1)
    west = pltpu.roll(index, 1, 1)
    east = pltpu.roll(index, LANES - 1, 1)
    south = jnp.where(row == 0, -1, pltpu.roll(index, 1, 0))
    north = jnp.where(row == rows - 1, -1, pltpu.roll(index, rows - 1, 0))
    col = jnp.where(sea, lane, -1)
    shift = jnp.where(sea, lane - rank, 0)
    for bit in range(7):
        width = 1 << bit
        col_m = pltpu.roll(col, LANES - width, 1)
        shift_m = pltpu.roll(shift, LANES - width, 1)
        take = (col_m >= 0) & (((shift_m >> bit) & 1) == 1)
        stay = (col >= 0) & (((shift >> bit) & 1) == 0)
        col = jnp.where(take, col_m, jnp.where(stay, col, -1))
        shift = jnp.where(take, shift_m, shift)
    source_col = jnp.maximum(lane_take(col, (lane - begin) & (LANES - 1)), 0)
    for i, table in enumerate((west, east, south, north)):
        rolled[i] = lane_take(table, source_col)
    rolled[4] = begin
    rolled[5] = begin + count

    q_tile = lax.broadcasted_iota(jnp.int32, (tiles, LANES), 0)
    q_lane = lax.broadcasted_iota(jnp.int32, (tiles, LANES), 1)
    q = q_tile * LANES + q_lane

    def spread(r, carry):
        at = pl.ds(r, 1)
        inside = (q >= rolled[4, at, :]) & (q < rolled[5, at, :])
        pieces = [jnp.where(inside, rolled[i, at, :], carry[i]) for i in range(4)]
        return (*pieces, jnp.where(inside, lat[at, :], carry[4]))

    zero = jnp.zeros((tiles, LANES), jnp.int32)
    found = lax.fori_loop(0, rows, spread, (zero, zero, zero, zero, zero.astype(jnp.float32)))
    order = (q_lane & (granule - 1)) * n + q_lane // granule
    for i in range(4):
        near = found[i]
        code = (((near >> 7) - q_tile + 1) * LANES + granule * (near & (n - 1))
                + ((near & (LANES - 1)) >> log_n))
        code = lane_take(jnp.where(near < 0, 3 * LANES, code), order)
        for t in range(tiles):
            tabs[t, i] = jnp.broadcast_to(code[t:t + 1, :], (8, LANES))
    inverse_lat = lane_take(found[4], order)
    for t in range(tiles):
        lat_tab[t] = jnp.broadcast_to(inverse_lat[t:t + 1, :], (8, LANES))

    lane8 = lax.broadcasted_iota(jnp.int32, (8, LANES), 1)

    def advance(src, dst, sub, first_row):
        at = pl.ds(8 * sub, 8)
        for h in range(halves):
            part = pl.ds(h * LANES, LANES)
            moved = granule_transpose([src[d, at, part] for d in range(n)], granule, lane8)
            for t in range(n):
                grid[sub, h * n + t] = moved[t]
        zonal = along[rows_of(first_row, 8), :]
        merid = across[rows_of(first_row, 8), :]
        from_west = zonal > 0.0
        from_south = merid > 0.0
        zonal, merid = jnp.abs(zonal), jnp.abs(merid)

        def pick(code, prev, cur, nxt):
            where = code & (LANES - 1)
            tile = code >> 7
            got = jnp.where(tile == 1, lane_take(cur, where), 0.0)
            got = jnp.where(tile == 0, lane_take(prev, where), got)
            return jnp.where(tile == 2, lane_take(nxt, where), got)

        for h in range(halves):
            new = []
            for u in range(n):
                t = h * n + u
                prev, cur, nxt = grid[sub, max(t - 1, 0)], grid[sub, t], grid[sub, min(t + 1, tiles - 1)]
                beside = pick(jnp.where(from_west, tabs[t, 0], tabs[t, 1]), prev, cur, nxt)
                behind = pick(jnp.where(from_south, tabs[t, 2], tabs[t, 3]), prev, cur, nxt)
                new.append(cur - zonal * lat_tab[t] * (cur - beside) - merid * (cur - behind))
            moved = granule_transpose(new, granule, lane8)
            part = pl.ds(h * LANES, LANES)
            for d in range(n):
                dst[d, at, part] = moved[d]

    if extra:
        @pl.when(me < extra)
        def _():
            wait_bytes(ex_in.at[others], exf_recv)
            advance(ex_in, ex_out, 0, 8 * me)
            each_peer(lambda p: remote(ex_out.at[p], out.at[rows_of(8 * me, 8)], exb_send, exb_recv.at[me], p).start())
            out[rows_of(8 * me, 8), :] = ex_out[me]

    def one_chunk(c, carry):
        wait_bytes(arrived.at[c, others], fwd_recv.at[c])
        mine = base + c * CHUNK * n + CHUNK * me
        for sub in range(CHUNK // 8):
            advance(arrived.at[c], result.at[c], sub, mine + 8 * sub)
        each_peer(lambda p: remote(result.at[c, p], out.at[rows_of(mine, CHUNK)],
                                   back_send.at[c], back_recv.at[c], p).start())
        out[rows_of(mine, CHUNK), :] = result[c, me]
        return carry

    lax.fori_loop(0, chunks, one_chunk, 0)

    wait_bytes(slots.at[others], mask_send)
    for c in range(chunks):
        wait_bytes(arrived.at[c, others], fwd_send.at[c])
        wait_bytes(result.at[c, others], back_send.at[c])
        wait_bytes(result.at[c, others], back_recv.at[c])
    if extra:
        for p in range(extra):
            @pl.when(me != p)
            def _():
                wait_bytes(ex_in.at[0], exf_send.at[p])
                wait_bytes(ex_in.at[0], exb_recv.at[p])

        @pl.when(me < extra)
        def _():
            wait_bytes(ex_out.at[others], exb_send)


def shards(n, spectrum, wind_speed, wind_dir, turning, sea_mask, band_start):
    comps, points = spectrum.shape
    band_rows = sea_mask.shape[0]
    rows = band_rows * n
    tiles = points * n // LANES
    groups = comps // 8
    chunks = max(groups // n * 8 // CHUNK, 1)
    extra = max(groups - n * (groups // n), 1)
    latitude = (-60.0 + 120.0 * (np.arange(rows) + 0.5) / rows) * (math.pi / 180.0)
    lat = np.ascontiguousarray(np.broadcast_to((1.0 / np.cos(latitude))[:, None], (rows, LANES))).astype(np.float32)
    vmem = pl.BlockSpec(memory_space=pltpu.VMEM)
    dma = pltpu.SemaphoreType.DMA
    f32, i32 = jnp.float32, jnp.int32
    line = lambda v: v.reshape(1, points)
    operands = (spectrum, line(wind_speed), line(wind_dir), line(turning), sea_mask, *spectral_tables(), lat)
    call = pl.pallas_call(
        functools.partial(kernel, n),
        out_shape=jax.ShapeDtypeStruct((comps, points), f32),
        in_specs=[pl.BlockSpec(memory_space=pltpu.HBM)] * 11,
        out_specs=vmem,
        scratch_shapes=[
            *(pltpu.VMEM(x.shape, x.dtype) for x in operands),
            dma((11,)),
            pltpu.VMEM((comps, points), f32),
            pltpu.VMEM((chunks, n, CHUNK, points), f32),
            pltpu.VMEM((chunks, n, CHUNK, points), f32),
            pltpu.VMEM((n, 8, points), f32),
            pltpu.VMEM((n, 8, points), f32),
            pltpu.VMEM((PAIR, points), f32),
            pltpu.VMEM((n, 8, LANES), f32),
            pltpu.VMEM((rows, LANES), f32),
            pltpu.VMEM((6, rows, LANES), i32),
            pltpu.VMEM((tiles, 4, 8, LANES), i32),
            pltpu.VMEM((tiles, 8, LANES), f32),
            pltpu.VMEM((CHUNK // 8, tiles, 8, LANES), f32),
            dma, dma,
            dma((chunks,)), dma((chunks,)), dma((chunks,)), dma((chunks,)),
            dma((extra,)), dma, dma, dma((extra,)),
        ],
        compiler_params=pltpu.CompilerParams(
            collective_id=0, has_side_effects=True, vmem_limit_bytes=60 * 1024 * 1024
        ),
    )
    return call(*operands)


def solution(mesh):
    placed = (
        P(None, ("grp", "pts")),
        P(("grp", "pts")),
        P(("grp", "pts")),
        P(("grp", "pts")),
        P("pts", None),
        P(),
    )
    return jax.shard_map(
        functools.partial(shards, mesh.shape["pts"]), mesh=mesh, in_specs=placed,
        out_specs=P(None, ("grp", "pts")), check_vma=False
    )
```

```python
import functools
import math

import jax
import jax.numpy as jnp
import numpy as np
from jax import lax
from jax.experimental import pallas as pl
from jax.experimental.pallas import tpu as pltpu
from jax.sharding import PartitionSpec as P

DIRS = 36
FREQS = 36
PAIR = 2 * DIRS
LANES = 128
CHUNK = 16
MESH = pl.DeviceIdType.MESH


def spectral_tables():
    heading = 2.0 * np.pi / DIRS * np.arange(DIRS)
    group_speed = 0.3 + 0.5 * np.arange(FREQS) / (FREQS - 1)
    along = ((0.4 * group_speed)[:, None] * np.cos(heading)[None, :]).reshape(-1, 1)
    across = ((0.35 * group_speed)[:, None] * np.sin(heading)[None, :]).reshape(-1, 1)
    wide = lambda v, lanes: np.ascontiguousarray(np.broadcast_to(v, (v.shape[0], lanes))).astype(np.float32)
    cos2 = np.tile(np.cos(heading), 2)[:, None]
    sin2 = np.tile(np.sin(heading), 2)[:, None]
    ids = np.arange(DIRS)
    turn = 0.5 * (ids[None, :] == (ids[:, None] + 1) % DIRS) - 0.5 * (ids[None, :] == (ids[:, None] - 1) % DIRS)
    turn2 = np.kron(np.eye(2), turn).astype(np.float32)
    return wide(along, LANES), wide(across, LANES), wide(cos2, LANES), wide(sin2, LANES), turn2


def lane_take(x, idx):
    return jnp.take_along_axis(x, idx, axis=1, mode="promise_in_bounds")


def granule_transpose(tiles, granule, lane):
    tiles = list(tiles)
    step = 1
    while step < len(tiles):
        keep = (lane // granule) & step == 0
        for d in range(len(tiles)):
            if d & step == 0:
                a, b = tiles[d], tiles[d | step]
                width = step * granule
                tiles[d] = jnp.where(keep, a, pltpu.roll(b, width, 1))
                tiles[d | step] = jnp.where(keep, pltpu.roll(a, LANES - width, 1), b)
        step *= 2
    return tiles


def kernel(n, spec_hbm, speed_hbm, wdir_hbm, turning_hbm, mask_hbm, along_hbm, across_hbm, cos2_hbm, sin2_hbm,
           turn2_hbm, lat_hbm, out, spec, speed, wdir, turning, mask, along, across, cos2, sin2, turn2, lat, loaded, refr, arrived, result, ex_in, ex_out, aligned, slots, cells, rolled, tabs, lat_tab, grid,
           mask_send, mask_recv, fwd_send, fwd_recv, back_send, back_recv,
           exf_send, exf_recv, exb_send, exb_recv, own):
    me = lax.axis_index("pts")
    comps, points = spec.shape
    band_rows = mask.shape[0]
    rows = band_rows * n
    tiles = points * n // LANES
    halves = points // LANES
    granule = LANES // n
    log_n = n.bit_length() - 1
    groups = comps // 8
    per_dev = groups // n * 8
    chunks = per_dev // CHUNK
    extra = groups - n * (per_dev // 8)
    base = 8 * extra

    half = n // 2
    operands = {
        "mask": (mask_hbm, mask), "speed": (speed_hbm, speed), "wdir": (wdir_hbm, wdir),
        "turning": (turning_hbm, turning), "spec": (spec_hbm, spec), "cos2": (cos2_hbm, cos2),
        "sin2": (sin2_hbm, sin2), "turn2": (turn2_hbm, turn2), "lat": (lat_hbm, lat),
        "along": (along_hbm, along), "across": (across_hbm, across),
    }
    loads = {name: pltpu.make_async_copy(src, dst, loaded.at[i]) for i, (name, (src, dst)) in enumerate(operands.items())}
    for load in loads.values():
        load.start()

    def need(*names):
        for name in names:
            loads[name].wait()

    def each_peer(body):
        def far(i, carry):
            body(half * (1 - me // half) + lax.rem(me + i, half))
            return carry

        def near(i, carry):
            body(half * (me // half) + lax.rem(me + i, half))
            return carry

        lax.fori_loop(0, half, far, 0)
        lax.fori_loop(1, half, near, 0)

    def remote(src, dst, send, recv, dev):
        return pltpu.make_async_remote_copy(src_ref=src, dst_ref=dst, send_sem=send, recv_sem=recv,
                                            device_id={"pts": dev}, device_id_type=MESH)

    def wait_bytes(ref, sem):
        pltpu.make_async_copy(ref, ref, sem).wait()

    def rows_of(start, count):
        return pl.ds(pl.multiple_of(start, 8), count)

    barrier = pltpu.get_barrier_semaphore()
    each_peer(lambda p: pl.semaphore_signal(barrier, inc=1, device_id={"pts": p}, device_id_type=MESH))
    need("mask")
    slots[me] = jnp.zeros((8, LANES), jnp.float32)
    slots[me, 0:band_rows, :] = mask[...].astype(jnp.float32)

    need("speed", "wdir", "turning", "cos2", "sin2", "turn2")
    cos_w = speed[...] * jnp.cos(wdir[...])
    sin_w = speed[...] * jnp.sin(wdir[...])
    aligned[...] = cos2[:, 0:1] * cos_w + sin2[:, 0:1] * sin_w
    need("spec")
    energy = jnp.sum(spec[...].reshape(comps // 8, 8, points), axis=0)
    energy = jnp.sum(energy, axis=0, keepdims=True) * (0.1 / comps)
    turn_col = turning[...]
    second = lax.broadcasted_iota(jnp.int32, (PAIR, points), 0) >= DIRS

    pl.semaphore_wait(barrier, n - 1)
    each_peer(lambda p: remote(slots.at[me], slots.at[me], mask_send, mask_recv, p).start())

    def source(i, carry):
        at = rows_of(i * PAIR, PAIR)
        freq = 0.5 + (3.0 / (FREQS - 1)) * i.astype(jnp.float32)
        sigma = jnp.where(second, freq + 1.5 / (FREQS - 1), freq)
        inv = 1.0 / sigma
        growth = 0.2 * jnp.maximum(aligned[...] * inv - 0.3, 0.0)
        x = spec[at, :] * jnp.exp(growth - sigma * energy)
        rot = jnp.dot(turn2[...], x, precision=lax.Precision.HIGHEST, preferred_element_type=jnp.float32)
        refr[at, :] = x - turn_col * inv * rot
        return carry

    done = 0

    def source_to(row_end, done):
        end = -(-row_end // PAIR)
        if end > done:
            lax.fori_loop(done, end, source, 0)
        return max(end, done)

    done = source_to(base, done)
    for p in range(extra):
        @pl.when(me != p)
        def _():
            remote(refr.at[pl.ds(8 * p, 8)], ex_in.at[me], exf_send.at[p], exf_recv, p).start()

        @pl.when(me == p)
        def _():
            ex_in[me] = refr[8 * p:8 * p + 8, :]
    for c in range(chunks):
        first = base + c * CHUNK * n
        done = source_to(first + CHUNK * n, done)
        each_peer(lambda p: remote(refr.at[rows_of(first + CHUNK * p, CHUNK)], arrived.at[c, me],
                                   fwd_send.at[c], fwd_recv.at[c], p).start())
        arrived[c, me] = refr[rows_of(first + CHUNK * me, CHUNK), :]

    need("lat", "along", "across")
    others = pl.ds(0, n - 1)
    wait_bytes(slots.at[others], mask_recv)
    for b in range(n):
        cells[band_rows * b:band_rows * (b + 1), :] = slots[b, 0:band_rows, :]
    m = cells[...]
    tri = (lax.broadcasted_iota(jnp.int32, (LANES, LANES), 0)
           < lax.broadcasted_iota(jnp.int32, (LANES, LANES), 1)).astype(jnp.float32)
    low = (lax.broadcasted_iota(jnp.int32, (rows, rows), 1)
           < lax.broadcasted_iota(jnp.int32, (rows, rows), 0)).astype(jnp.float32)
    rank = jnp.dot(m, tri, preferred_element_type=jnp.float32).astype(jnp.int32)
    before = jnp.dot(low, m, preferred_element_type=jnp.float32)
    begin = jnp.broadcast_to(jnp.sum(before, axis=1, keepdims=True), m.shape).astype(jnp.int32)
    count = jnp.broadcast_to(jnp.sum(m, axis=1, keepdims=True), m.shape).astype(jnp.int32)
    sea = m > 0.5
    lane = lax.broadcasted_iota(jnp.int32, (rows, LANES), 1)
    row = lax.broadcasted_iota(jnp.int32, (rows, LANES), 0)
    index = jnp.where(sea, begin + rank, -1)
    west = pltpu.roll(index, 1, 1)
    east = pltpu.roll(index, LANES - 1, 1)
    south = jnp.where(row == 0, -1, pltpu.roll(index, 1, 0))
    north = jnp.where(row == rows - 1, -1, pltpu.roll(index, rows - 1, 0))
    col = jnp.where(sea, lane, -1)
    shift = jnp.where(sea, lane - rank, 0)
    for bit in range(7):
        width = 1 << bit
        col_m = pltpu.roll(col, LANES - width, 1)
        shift_m = pltpu.roll(shift, LANES - width, 1)
        take = (col_m >= 0) & (((shift_m >> bit) & 1) == 1)
        stay = (col >= 0) & (((shift >> bit) & 1) == 0)
        col = jnp.where(take, col_m, jnp.where(stay, col, -1))
        shift = jnp.where(take, shift_m, shift)
    source_col = jnp.maximum(lane_take(col, (lane - begin) & (LANES - 1)), 0)
    for i, table in enumerate((west, east, south, north)):
        rolled[i] = lane_take(table, source_col)
    rolled[4] = begin
    rolled[5] = begin + count

    q_tile = lax.broadcasted_iota(jnp.int32, (tiles, LANES), 0)
    q_lane = lax.broadcasted_iota(jnp.int32, (tiles, LANES), 1)
    q = q_tile * LANES + q_lane

    def spread(r, carry):
        at = pl.ds(r, 1)
        inside = (q >= rolled[4, at, :]) & (q < rolled[5, at, :])
        pieces = [jnp.where(inside, rolled[i, at, :], carry[i]) for i in range(4)]
        return (*pieces, jnp.where(inside, lat[at, :], carry[4]))

    zero = jnp.zeros((tiles, LANES), jnp.int32)
    found = lax.fori_loop(0, rows, spread, (zero, zero, zero, zero, zero.astype(jnp.float32)))
    order = (q_lane & (granule - 1)) * n + q_lane // granule
    for i in range(4):
        near = found[i]
        code = (((near >> 7) - q_tile + 1) * LANES + granule * (near & (n - 1))
                + ((near & (LANES - 1)) >> log_n))
        code = lane_take(jnp.where(near < 0, 3 * LANES, code), order)
        for t in range(tiles):
            tabs[t, i] = jnp.broadcast_to(code[t:t + 1, :], (8, LANES))
    inverse_lat = lane_take(found[4], order)
    for t in range(tiles):
        lat_tab[t] = jnp.broadcast_to(inverse_lat[t:t + 1, :], (8, LANES))

    lane8 = lax.broadcasted_iota(jnp.int32, (8, LANES), 1)

    def advance(src, dst, sub, first_row):
        at = pl.ds(8 * sub, 8)
        for h in range(halves):
            part = pl.ds(h * LANES, LANES)
            moved = granule_transpose([src[d, at, part] for d in range(n)], granule, lane8)
            for t in range(n):
                grid[sub, h * n + t] = moved[t]
        zonal = along[rows_of(first_row, 8), :]
        merid = across[rows_of(first_row, 8), :]
        from_west = zonal > 0.0
        from_south = merid > 0.0
        zonal, merid = jnp.abs(zonal), jnp.abs(merid)

        def pick(code, prev, cur, nxt):
            where = code & (LANES - 1)
            tile = code >> 7
            got = jnp.where(tile == 1, lane_take(cur, where), 0.0)
            got = jnp.where(tile == 0, lane_take(prev, where), got)
            return jnp.where(tile == 2, lane_take(nxt, where), got)

        for h in range(halves):
            new = []
            for u in range(n):
                t = h * n + u
                prev, cur, nxt = grid[sub, max(t - 1, 0)], grid[sub, t], grid[sub, min(t + 1, tiles - 1)]
                beside = pick(jnp.where(from_west, tabs[t, 0], tabs[t, 1]), prev, cur, nxt)
                behind = pick(jnp.where(from_south, tabs[t, 2], tabs[t, 3]), prev, cur, nxt)
                new.append(cur - zonal * lat_tab[t] * (cur - beside) - merid * (cur - behind))
            moved = granule_transpose(new, granule, lane8)
            part = pl.ds(h * LANES, LANES)
            for d in range(n):
                dst[d, at, part] = moved[d]

    if extra:
        @pl.when(me < extra)
        def _():
            wait_bytes(ex_in.at[others], exf_recv)
            advance(ex_in, ex_out, 0, 8 * me)
            each_peer(lambda p: remote(ex_out.at[p], out.at[rows_of(8 * me, 8)], exb_send, exb_recv.at[me], p).start())
            pltpu.make_async_copy(ex_out.at[me], out.at[rows_of(8 * me, 8)], own.at[chunks]).start()

    def one_chunk(c, carry):
        wait_bytes(arrived.at[c, others], fwd_recv.at[c])
        mine = base + c * CHUNK * n + CHUNK * me
        for sub in range(CHUNK // 8):
            advance(arrived.at[c], result.at[c], sub, mine + 8 * sub)
        each_peer(lambda p: remote(result.at[c, p], out.at[rows_of(mine, CHUNK)],
                                   back_send.at[c], back_recv.at[c], p).start())
        pltpu.make_async_copy(result.at[c, me], out.at[rows_of(mine, CHUNK)], own.at[c]).start()
        return carry

    lax.fori_loop(0, chunks, one_chunk, 0)

    wait_bytes(slots.at[others], mask_send)
    for c in range(chunks):
        wait_bytes(arrived.at[c, others], fwd_send.at[c])
        wait_bytes(result.at[c, others], back_send.at[c])
        wait_bytes(result.at[c, others], back_recv.at[c])
        wait_bytes(result.at[c, 0], own.at[c])
    if extra:
        for p in range(extra):
            @pl.when(me != p)
            def _():
                wait_bytes(ex_in.at[0], exf_send.at[p])
                wait_bytes(ex_in.at[0], exb_recv.at[p])

        @pl.when(me < extra)
        def _():
            wait_bytes(ex_out.at[others], exb_send)
            wait_bytes(ex_out.at[0], own.at[chunks])


def shards(n, spectrum, wind_speed, wind_dir, turning, sea_mask, band_start):
    comps, points = spectrum.shape
    band_rows = sea_mask.shape[0]
    rows = band_rows * n
    tiles = points * n // LANES
    groups = comps // 8
    chunks = max(groups // n * 8 // CHUNK, 1)
    extra = max(groups - n * (groups // n), 1)
    latitude = (-60.0 + 120.0 * (np.arange(rows) + 0.5) / rows) * (math.pi / 180.0)
    lat = np.ascontiguousarray(np.broadcast_to((1.0 / np.cos(latitude))[:, None], (rows, LANES))).astype(np.float32)
    dma = pltpu.SemaphoreType.DMA
    f32, i32 = jnp.float32, jnp.int32
    line = lambda v: v.reshape(1, points)
    operands = (spectrum, line(wind_speed), line(wind_dir), line(turning), sea_mask, *spectral_tables(), lat)
    call = pl.pallas_call(
        functools.partial(kernel, n),
        out_shape=jax.ShapeDtypeStruct((comps, points), f32),
        in_specs=[pl.BlockSpec(memory_space=pltpu.HBM)] * 11,
        out_specs=pl.BlockSpec(memory_space=pl.ANY),
        scratch_shapes=[
            *(pltpu.VMEM(x.shape, x.dtype) for x in operands),
            dma((11,)),
            pltpu.VMEM((comps, points), f32),
            pltpu.VMEM((chunks, n, CHUNK, points), f32),
            pltpu.VMEM((chunks, n, CHUNK, points), f32),
            pltpu.VMEM((n, 8, points), f32),
            pltpu.VMEM((n, 8, points), f32),
            pltpu.VMEM((PAIR, points), f32),
            pltpu.VMEM((n, 8, LANES), f32),
            pltpu.VMEM((rows, LANES), f32),
            pltpu.VMEM((6, rows, LANES), i32),
            pltpu.VMEM((tiles, 4, 8, LANES), i32),
            pltpu.VMEM((tiles, 8, LANES), f32),
            pltpu.VMEM((CHUNK // 8, tiles, 8, LANES), f32),
            dma, dma,
            dma((chunks,)), dma((chunks,)), dma((chunks,)), dma((chunks,)),
            dma((extra,)), dma, dma, dma((extra,)), dma((chunks + 1,)),
        ],
        compiler_params=pltpu.CompilerParams(
            collective_id=0, has_side_effects=True, vmem_limit_bytes=60 * 1024 * 1024
        ),
    )
    return call(*operands)


def solution(mesh):
    placed = (
        P(None, ("grp", "pts")),
        P(("grp", "pts")),
        P(("grp", "pts")),
        P(("grp", "pts")),
        P("pts", None),
        P(),
    )
    return jax.shard_map(
        functools.partial(shards, mesh.shape["pts"]), mesh=mesh, in_specs=placed,
        out_specs=P(None, ("grp", "pts")), check_vma=False
    )
```

```python
import functools
import math

import jax
import jax.numpy as jnp
import numpy as np
from jax import lax
from jax.experimental import pallas as pl
from jax.experimental.pallas import tpu as pltpu
from jax.sharding import PartitionSpec as P

DIRS = 36
FREQS = 36
PAIR = 2 * DIRS
LANES = 128
CHUNK = 16
MESH = pl.DeviceIdType.MESH


def spectral_tables():
    heading = 2.0 * np.pi / DIRS * np.arange(DIRS)
    group_speed = 0.3 + 0.5 * np.arange(FREQS) / (FREQS - 1)
    along = ((0.4 * group_speed)[:, None] * np.cos(heading)[None, :]).reshape(-1, 1)
    across = ((0.35 * group_speed)[:, None] * np.sin(heading)[None, :]).reshape(-1, 1)
    wide = lambda v, lanes: np.ascontiguousarray(np.broadcast_to(v, (v.shape[0], lanes))).astype(np.float32)
    cos2 = np.tile(np.cos(heading), 2)[:, None]
    sin2 = np.tile(np.sin(heading), 2)[:, None]
    ids = np.arange(DIRS)
    turn = 0.5 * (ids[None, :] == (ids[:, None] + 1) % DIRS) - 0.5 * (ids[None, :] == (ids[:, None] - 1) % DIRS)
    turn2 = np.kron(np.eye(2), turn).astype(np.float32)
    return wide(along, LANES), wide(across, LANES), wide(cos2, LANES), wide(sin2, LANES), turn2


def lane_take(x, idx):
    return jnp.take_along_axis(x, idx, axis=1, mode="promise_in_bounds")


def granule_transpose(tiles, granule, lane):
    tiles = list(tiles)
    step = 1
    while step < len(tiles):
        keep = (lane // granule) & step == 0
        for d in range(len(tiles)):
            if d & step == 0:
                a, b = tiles[d], tiles[d | step]
                width = step * granule
                tiles[d] = jnp.where(keep, a, pltpu.roll(b, width, 1))
                tiles[d | step] = jnp.where(keep, pltpu.roll(a, LANES - width, 1), b)
        step *= 2
    return tiles


def kernel(n, spec_hbm, speed_hbm, wdir_hbm, turning_hbm, mask_hbm, along_hbm, across_hbm, cos2_hbm, sin2_hbm,
           turn2_hbm, lat_hbm, out, spec, speed, wdir, turning, mask, along, across, cos2, sin2, turn2, lat, loaded, refr, arrived, result, ex_in, ex_out, aligned, slots, cells, rolled, tabs, lat_tab, grid,
           mask_send, mask_recv, fwd_send, fwd_recv, back_send, back_recv,
           exf_send, exf_recv, exb_send, exb_recv, own):
    me = lax.axis_index("pts")
    comps, points = spec.shape
    band_rows = mask.shape[0]
    rows = band_rows * n
    tiles = points * n // LANES
    halves = points // LANES
    granule = LANES // n
    log_n = n.bit_length() - 1
    groups = comps // 8
    per_dev = groups // n * 8
    chunks = per_dev // CHUNK
    extra = groups - n * (per_dev // 8)
    base = 8 * extra

    half = n // 2
    operands = {
        "mask": (mask_hbm, mask), "speed": (speed_hbm, speed), "wdir": (wdir_hbm, wdir),
        "turning": (turning_hbm, turning), "spec": (spec_hbm, spec), "cos2": (cos2_hbm, cos2),
        "sin2": (sin2_hbm, sin2), "turn2": (turn2_hbm, turn2), "lat": (lat_hbm, lat),
        "along": (along_hbm, along), "across": (across_hbm, across),
    }
    loads = {name: pltpu.make_async_copy(src, dst, loaded.at[i]) for i, (name, (src, dst)) in enumerate(operands.items())}
    for load in loads.values():
        load.start()

    def need(*names):
        for name in names:
            loads[name].wait()

    def each_peer(body):
        def far(i, carry):
            body(half * (1 - me // half) + lax.rem(me + i, half))
            return carry

        def near(i, carry):
            body(half * (me // half) + lax.rem(me + i, half))
            return carry

        lax.fori_loop(0, half, far, 0)
        lax.fori_loop(1, half, near, 0)

    def remote(src, dst, send, recv, dev):
        return pltpu.make_async_remote_copy(src_ref=src, dst_ref=dst, send_sem=send, recv_sem=recv,
                                            device_id={"pts": dev}, device_id_type=MESH)

    def wait_bytes(ref, sem):
        pltpu.make_async_copy(ref, ref, sem).wait()

    def rows_of(start, count):
        return pl.ds(pl.multiple_of(start, 8), count)

    barrier = pltpu.get_barrier_semaphore()
    each_peer(lambda p: pl.semaphore_signal(barrier, inc=1, device_id={"pts": p}, device_id_type=MESH))
    need("mask")
    slots[me] = jnp.zeros((8, LANES), jnp.float32)
    slots[me, 0:band_rows, :] = mask[...].astype(jnp.float32)

    need("speed", "wdir", "turning", "cos2", "sin2", "turn2")
    cos_w = speed[...] * jnp.cos(wdir[...])
    sin_w = speed[...] * jnp.sin(wdir[...])
    aligned[...] = cos2[:, 0:1] * cos_w + sin2[:, 0:1] * sin_w
    need("spec")
    energy = jnp.sum(spec[...].reshape(comps // 8, 8, points), axis=0)
    energy = jnp.sum(energy, axis=0, keepdims=True) * (0.1 / comps)
    turn_col = turning[...]
    second = lax.broadcasted_iota(jnp.int32, (PAIR, points), 0) >= DIRS

    pl.semaphore_wait(barrier, n - 1)
    each_peer(lambda p: remote(slots.at[me], slots.at[me], mask_send, mask_recv, p).start())

    def source(i, carry):
        at = rows_of(i * PAIR, PAIR)
        freq = 0.5 + (3.0 / (FREQS - 1)) * i.astype(jnp.float32)
        sigma = jnp.where(second, freq + 1.5 / (FREQS - 1), freq)
        inv = 1.0 / sigma
        growth = 0.2 * jnp.maximum(aligned[...] * inv - 0.3, 0.0)
        x = spec[at, :] * jnp.exp(growth - sigma * energy)
        rot = jnp.dot(turn2[...], x, precision=lax.Precision.HIGHEST, preferred_element_type=jnp.float32)
        refr[at, :] = x - turn_col * inv * rot
        return carry

    done = 0

    def source_to(row_end, done):
        end = -(-row_end // PAIR)
        if end > done:
            lax.fori_loop(done, end, source, 0)
        return max(end, done)

    done = source_to(base, done)
    for p in range(extra):
        @pl.when(me != p)
        def _():
            remote(refr.at[pl.ds(8 * p, 8)], ex_in.at[me], exf_send.at[p], exf_recv, p).start()

        @pl.when(me == p)
        def _():
            ex_in[me] = refr[8 * p:8 * p + 8, :]
    for c in range(chunks):
        first = base + c * CHUNK * n
        done = source_to(first + CHUNK * n, done)
        each_peer(lambda p: remote(refr.at[rows_of(first + CHUNK * p, CHUNK)], arrived.at[c, me],
                                   fwd_send.at[c], fwd_recv.at[c], p).start())
        arrived[c, me] = refr[rows_of(first + CHUNK * me, CHUNK), :]

    need("lat", "along", "across")
    others = pl.ds(0, n - 1)
    wait_bytes(slots.at[others], mask_recv)
    for b in range(n):
        cells[band_rows * b:band_rows * (b + 1), :] = slots[b, 0:band_rows, :]
    m = cells[...]
    tri = (lax.broadcasted_iota(jnp.int32, (LANES, LANES), 0)
           < lax.broadcasted_iota(jnp.int32, (LANES, LANES), 1)).astype(jnp.float32)
    low = (lax.broadcasted_iota(jnp.int32, (rows, rows), 1)
           < lax.broadcasted_iota(jnp.int32, (rows, rows), 0)).astype(jnp.float32)
    rank = jnp.dot(m, tri, preferred_element_type=jnp.float32).astype(jnp.int32)
    before = jnp.dot(low, m, preferred_element_type=jnp.float32)
    begin = jnp.broadcast_to(jnp.sum(before, axis=1, keepdims=True), m.shape).astype(jnp.int32)
    count = jnp.broadcast_to(jnp.sum(m, axis=1, keepdims=True), m.shape).astype(jnp.int32)
    sea = m > 0.5
    lane = lax.broadcasted_iota(jnp.int32, (rows, LANES), 1)
    row = lax.broadcasted_iota(jnp.int32, (rows, LANES), 0)
    index = jnp.where(sea, begin + rank, -1)
    west = pltpu.roll(index, 1, 1)
    east = pltpu.roll(index, LANES - 1, 1)
    south = jnp.where(row == 0, -1, pltpu.roll(index, 1, 0))
    north = jnp.where(row == rows - 1, -1, pltpu.roll(index, rows - 1, 0))
    col = jnp.where(sea, lane, -1)
    shift = jnp.where(sea, lane - rank, 0)
    for bit in range(7):
        width = 1 << bit
        col_m = pltpu.roll(col, LANES - width, 1)
        shift_m = pltpu.roll(shift, LANES - width, 1)
        take = (col_m >= 0) & (((shift_m >> bit) & 1) == 1)
        stay = (col >= 0) & (((shift >> bit) & 1) == 0)
        col = jnp.where(take, col_m, jnp.where(stay, col, -1))
        shift = jnp.where(take, shift_m, shift)
    source_col = jnp.maximum(lane_take(col, (lane - begin) & (LANES - 1)), 0)
    for i, table in enumerate((west, east, south, north)):
        rolled[i] = lane_take(table, source_col)
    rolled[4] = begin
    rolled[5] = begin + count

    q_tile = lax.broadcasted_iota(jnp.int32, (tiles, LANES), 0)
    q_lane = lax.broadcasted_iota(jnp.int32, (tiles, LANES), 1)
    q = q_tile * LANES + q_lane

    def spread(r, carry):
        at = pl.ds(r, 1)
        inside = (q >= rolled[4, at, :]) & (q < rolled[5, at, :])
        pieces = [jnp.where(inside, rolled[i, at, :], carry[i]) for i in range(4)]
        return (*pieces, jnp.where(inside, lat[at, :], carry[4]))

    zero = jnp.zeros((tiles, LANES), jnp.int32)
    found = lax.fori_loop(0, rows, spread, (zero, zero, zero, zero, zero.astype(jnp.float32)))
    order = (q_lane & (granule - 1)) * n + q_lane // granule
    for i in range(4):
        near = found[i]
        code = (((near >> 7) - q_tile + 1) * LANES + granule * (near & (n - 1))
                + ((near & (LANES - 1)) >> log_n))
        code = lane_take(jnp.where(near < 0, 3 * LANES, code), order)
        for t in range(tiles):
            tabs[t, i] = jnp.broadcast_to(code[t:t + 1, :], (8, LANES))
    inverse_lat = lane_take(found[4], order)
    for t in range(tiles):
        lat_tab[t] = jnp.broadcast_to(inverse_lat[t:t + 1, :], (8, LANES))

    lane8 = lax.broadcasted_iota(jnp.int32, (8, LANES), 1)

    def advance(src, dst, sub, first_row):
        at = pl.ds(8 * sub, 8)
        for h in range(halves):
            part = pl.ds(h * LANES, LANES)
            moved = granule_transpose([src[d, at, part] for d in range(n)], granule, lane8)
            for t in range(n):
                grid[sub, h * n + t] = moved[t]
        zonal = along[rows_of(first_row, 8), :]
        merid = across[rows_of(first_row, 8), :]
        from_west = zonal > 0.0
        from_south = merid > 0.0
        zonal, merid = jnp.abs(zonal), jnp.abs(merid)

        def pick(code, prev, cur, nxt):
            where = code & (LANES - 1)
            tile = code >> 7
            got = jnp.where(tile == 1, lane_take(cur, where), 0.0)
            got = jnp.where(tile == 0, lane_take(prev, where), got)
            return jnp.where(tile == 2, lane_take(nxt, where), got)

        for h in range(halves):
            new = []
            for u in range(n):
                t = h * n + u
                prev, cur, nxt = grid[sub, max(t - 1, 0)], grid[sub, t], grid[sub, min(t + 1, tiles - 1)]
                beside = pick(jnp.where(from_west, tabs[t, 0], tabs[t, 1]), prev, cur, nxt)
                behind = pick(jnp.where(from_south, tabs[t, 2], tabs[t, 3]), prev, cur, nxt)
                new.append(cur - zonal * lat_tab[t] * (cur - beside) - merid * (cur - behind))
            moved = granule_transpose(new, granule, lane8)
            part = pl.ds(h * LANES, LANES)
            for d in range(n):
                dst[d, at, part] = moved[d]

    if extra:
        @pl.when(me < extra)
        def _():
            wait_bytes(ex_in.at[others], exf_recv)
            advance(ex_in, ex_out, 0, 8 * me)
            each_peer(lambda p: remote(ex_out.at[p], out.at[rows_of(8 * me, 8)], exb_send, exb_recv.at[me], p).start())
            pltpu.make_async_copy(ex_out.at[me], out.at[rows_of(8 * me, 8)], own.at[chunks]).start()

    def one_chunk(c, carry):
        wait_bytes(arrived.at[c, others], fwd_recv.at[c])
        mine = base + c * CHUNK * n + CHUNK * me
        for sub in range(CHUNK // 8):
            advance(arrived.at[c], result.at[c], sub, mine + 8 * sub)
        each_peer(lambda p: remote(result.at[c, p], out.at[rows_of(mine, CHUNK)],
                                   back_send.at[c], back_recv.at[c], p).start())
        pltpu.make_async_copy(result.at[c, me], out.at[rows_of(mine, CHUNK)], own.at[c]).start()
        return carry

    lax.fori_loop(0, chunks, one_chunk, 0)

    wait_bytes(slots.at[others], mask_send)
    for c in range(chunks):
        wait_bytes(arrived.at[c, others], fwd_send.at[c])
        wait_bytes(result.at[c, others], back_send.at[c])
        wait_bytes(result.at[c, others], back_recv.at[c])
        wait_bytes(result.at[c, 0], own.at[c])
    if extra:
        for p in range(extra):
            @pl.when(me != p)
            def _():
                wait_bytes(ex_in.at[0], exf_send.at[p])
                wait_bytes(ex_in.at[0], exb_recv.at[p])

        @pl.when(me < extra)
        def _():
            wait_bytes(ex_out.at[others], exb_send)
            wait_bytes(ex_out.at[0], own.at[chunks])


def shards(n, spectrum, wind_speed, wind_dir, turning, sea_mask, band_start):
    comps, points = spectrum.shape
    band_rows = sea_mask.shape[0]
    rows = band_rows * n
    tiles = points * n // LANES
    groups = comps // 8
    chunks = max(groups // n * 8 // CHUNK, 1)
    extra = max(groups - n * (groups // n), 1)
    latitude = (-60.0 + 120.0 * (np.arange(rows) + 0.5) / rows) * (math.pi / 180.0)
    lat = np.ascontiguousarray(np.broadcast_to((1.0 / np.cos(latitude))[:, None], (rows, LANES))).astype(np.float32)
    dma = pltpu.SemaphoreType.DMA
    f32, i32 = jnp.float32, jnp.int32
    line = lambda v: v.reshape(1, points)
    operands = (spectrum, line(wind_speed), line(wind_dir), line(turning), sea_mask, *spectral_tables(), lat)
    call = pl.pallas_call(
        functools.partial(kernel, n),
        out_shape=pltpu.VMEM((comps, points), f32),
        in_specs=[pl.BlockSpec(memory_space=pltpu.HBM)] * 11,
        out_specs=pl.BlockSpec(memory_space=pl.ANY),
        scratch_shapes=[
            *(pltpu.VMEM(x.shape, x.dtype) for x in operands),
            dma((11,)),
            pltpu.VMEM((comps, points), f32),
            pltpu.VMEM((chunks, n, CHUNK, points), f32),
            pltpu.VMEM((chunks, n, CHUNK, points), f32),
            pltpu.VMEM((n, 8, points), f32),
            pltpu.VMEM((n, 8, points), f32),
            pltpu.VMEM((PAIR, points), f32),
            pltpu.VMEM((n, 8, LANES), f32),
            pltpu.VMEM((rows, LANES), f32),
            pltpu.VMEM((6, rows, LANES), i32),
            pltpu.VMEM((tiles, 4, 8, LANES), i32),
            pltpu.VMEM((tiles, 8, LANES), f32),
            pltpu.VMEM((CHUNK // 8, tiles, 8, LANES), f32),
            dma, dma,
            dma((chunks,)), dma((chunks,)), dma((chunks,)), dma((chunks,)),
            dma((extra,)), dma, dma, dma((extra,)), dma((chunks + 1,)),
        ],
        compiler_params=pltpu.CompilerParams(
            collective_id=0, has_side_effects=True, vmem_limit_bytes=58 * 1024 * 1024
        ),
    )
    return call(*operands)


def solution(mesh):
    placed = (
        P(None, ("grp", "pts")),
        P(("grp", "pts")),
        P(("grp", "pts")),
        P(("grp", "pts")),
        P("pts", None),
        P(),
    )
    return jax.shard_map(
        functools.partial(shards, mesh.shape["pts"]), mesh=mesh, in_specs=placed,
        out_specs=P(None, ("grp", "pts")), check_vma=False
    )
```
